512 devices in a mesh: ta: 4 (over z_lo), gz: 16 (over z_hi, x), xy: 8 (over y, core).
Axes of the slice: x: 4, y: 4, z: 16 (z_hi: 4, z_lo: 4; z = z_hi * 4 + z_lo), core: 2. Of those that a mesh axis runs over, the one named last changes fastest.
Arguments:
- eigenvectors: bfloat16 [4, 128, 3, 2, 16, 1024], P('ta', ('gz', 'xy')), may hold values from -6 to 6
- gauge_links: bfloat16 [4, 3, 3, 2, 4, 16, 1024], P(None, None, None, None, 'ta', 'gz', 'xy'), may hold values from -2 to 2
- back_links: bfloat16 [4, 3, 3, 2, 4, 16, 1024], P(None, None, None, None, 'ta', 'gz', 'xy'), may hold values from -2 to 2, as said below
- clover: bfloat16 [2, 6, 6, 2, 4, 16, 1024], P(None, None, None, None, 'ta', 'gz', 'xy'), may hold values from -1.25 to 1.25
- source_eigen: int32 [32], replicated, may hold values from 0 to 127
- source_spin: int32 [32], replicated, may hold values from 0 to 3
- source_parity: int32 [32], replicated, may hold values from 0 to 1
Outputs:
- propagated: bfloat16 [32, 4, 3, 2, 4, 16, 1024], P(None, None, None, None, 'ta', 'gz', 'xy')
- projection: float32 [2, 4, 128, 128], P(None, 'ta')
The draws below stay inside these ranges and needn't reach their ends.
Inputs may be any that keep to these rules, and one draw needn't show every extreme that they name: back_links[d] at each site equals gauge_links[d] at the site one step below along direction d, periodically over the window.
All inputs are finite; a program needn't handle non-finite values.
Results may differ from the reference program's by a relative error of at most 0.0017.
Values may be sent and summed in bfloat16 or wider, within the bound.
No kernel may reach another device: no remote copies, remote signals or barrier semaphores. Data moves between devices by JAX's collectives and lax.ppermute only.
A program may use at most 64 MiB of HBM per device.

```python
import math
import jax
import jax.numpy as jnp
import numpy as np
from jax import lax

NEV = 128
NSRC = 32
NX = 64
NT = 4
NZ = 16
NY = 16


def shared_links(key):
    shape_full = (4, 3, 3, 2, NT, NZ, NY, NX)
    normal_part = jnp.clip(jax.random.normal(key, shape_full, jnp.float32), -5.0, 5.0) * 0.4
    return normal_part


def draw_gauge_links(key, part):
    return shared_links(key).reshape(4, 3, 3, 2, NT, NZ, NY * NX).astype(jnp.bfloat16)


def draw_back_links(key, part):
    base_links = shared_links(key)
    rolled = [jnp.roll(base_links[direction], 1, axis=6 - direction) for direction in range(4)]
    return jnp.stack(rolled).reshape(4, 3, 3, 2, NT, NZ, NY * NX).astype(jnp.bfloat16)


def touch_ends(entries, own_key, smallest, top_value):
    dims = entries.shape
    spot = [jax.random.randint(jax.random.fold_in(own_key, axis), (), 0, dims[axis]) for axis in range(len(dims))]
    entries = entries.at[tuple(spot)].set(smallest)
    longest = dims.index(max(dims))
    spot[longest] = (spot[longest] + 1) % dims[longest]
    return entries.at[tuple(spot)].set(top_value)


def block_scale(key, shape, shards, least, top_value):
    gain, own = 1.0, jax.random.fold_in(key, 6)
    for dim, blocks in shards:
        steps = jnp.exp(jax.random.uniform(jax.random.fold_in(own, dim), (blocks,), jnp.float32, least / len(shards), top_value / len(shards)))
        gain = gain * jnp.repeat(steps, shape[dim] // blocks).reshape([-1 if axis == dim else 1 for axis in range(len(shape))])
    return gain


def scatter_about(stream_key, shape, spread, reach, shards=(), kind=jnp.bfloat16):
    level = block_scale(stream_key, shape, shards, -0.22, 0.18) if shards else 1.0
    array = jax.random.normal(stream_key, shape, jnp.float32) * spread * level
    return jnp.minimum(jnp.maximum(array, -reach), reach).astype(kind)


def setup_inputs(seed: int = 0) -> dict:
    splits = jax.random.split(jax.random.key(seed), 8)
    eigenvectors = scatter_about(splits[0], (NT, NEV, 3, 2, NZ, NY * NX), 1.0, 6.0, ((0, 4), (1, 128)))
    gauge_links = draw_gauge_links(jax.random.fold_in(splits[7], 71), 0)
    back_links = draw_back_links(jax.random.fold_in(splits[7], 71), 0)
    clover = scatter_about(splits[3], (2, 6, 6, 2, NT, NZ, NY * NX), 0.2, 1.25, ((4, 4), (5, 16), (6, 8)))
    source_eigen = touch_ends(jax.random.randint(splits[4], (NSRC,), 0, NEV), jax.random.fold_in(splits[4], 1), 0, NEV - 1).astype(jnp.int32)
    source_spin = touch_ends(jax.random.randint(splits[5], (NSRC,), 0, 4), jax.random.fold_in(splits[5], 1), 0, 3).astype(jnp.int32)
    source_parity = touch_ends(jax.random.randint(splits[6], (NSRC,), 0, 2), jax.random.fold_in(splits[6], 1), 0, 1).astype(jnp.int32)
    return dict(eigenvectors=eigenvectors, gauge_links=gauge_links, back_links=back_links, clover=clover, source_eigen=source_eigen, source_spin=source_spin, source_parity=source_parity)


hopping = 0.125

def gamma_parts():
    real_part = np.zeros((4, 4, 4), np.float32)
    imag_part = np.zeros((4, 4, 4), np.float32)
    for direction, row_index, column_index, amount in ((0, 0, 3, 1.0), (0, 1, 2, 1.0), (0, 2, 1, -1.0), (0, 3, 0, -1.0), (2, 0, 2, 1.0), (2, 1, 3, -1.0), (2, 2, 0, -1.0), (2, 3, 1, 1.0)):
        imag_part[direction, row_index, column_index] = amount
    for direction, row_index, column_index, amount in ((1, 0, 3, -1.0), (1, 1, 2, 1.0), (1, 2, 1, 1.0), (1, 3, 0, -1.0), (3, 0, 2, 1.0), (3, 1, 3, 1.0), (3, 2, 0, 1.0), (3, 3, 1, 1.0)):
        real_part[direction, row_index, column_index] = amount
    return (real_part, imag_part)

def projectors(factor):
    real_part, imag_part = gamma_parts()
    identity = np.eye(4, dtype=np.float32)[None]
    return (jnp.asarray(identity + factor * real_part, jnp.float32), jnp.asarray(factor * imag_part, jnp.float32))

def color_apply(link_real, link_imag, values_real, values_imag, adjoint):
    if adjoint:
        link_real = jnp.swapaxes(link_real, 0, 1)
        link_imag = -jnp.swapaxes(link_imag, 0, 1)
    left_real = link_real[None, None]
    left_imag = link_imag[None, None]
    right_real = values_real[:, :, None]
    right_imag = values_imag[:, :, None]
    out_real = lax.optimization_barrier(jnp.sum(left_real * right_real - left_imag * right_imag, axis=3))
    out_imag = lax.optimization_barrier(jnp.sum(left_real * right_imag + left_imag * right_real, axis=3))
    return (out_real, out_imag)

def spin_apply(table_real, table_imag, values_real, values_imag):
    trailing = (1,) * (values_real.ndim - 2)
    left_real = table_real.reshape((1, 4, 4) + trailing)
    left_imag = table_imag.reshape((1, 4, 4) + trailing)
    right_real = values_real[:, None]
    right_imag = values_imag[:, None]
    out_real = lax.optimization_barrier(jnp.sum(left_real * right_real - left_imag * right_imag, axis=2))
    out_imag = lax.optimization_barrier(jnp.sum(left_real * right_imag + left_imag * right_real, axis=2))
    return (out_real, out_imag)

def clover_apply(clover, values_real, values_imag):
    shape_full = values_real.shape
    blocks_real = values_real.reshape((shape_full[0], 2, 6) + shape_full[3:])
    blocks_imag = values_imag.reshape((shape_full[0], 2, 6) + shape_full[3:])
    clover_real = clover[:, :, :, 0].astype(jnp.float32)[None]
    clover_imag = clover[:, :, :, 1].astype(jnp.float32)[None]
    right_real = blocks_real[:, :, None]
    right_imag = blocks_imag[:, :, None]
    out_real = lax.optimization_barrier(jnp.sum(clover_real * right_real - clover_imag * right_imag, axis=3))
    out_imag = lax.optimization_barrier(jnp.sum(clover_real * right_imag + clover_imag * right_real, axis=3))
    return (values_real + out_real.reshape(shape_full), values_imag + out_imag.reshape(shape_full))

def wilson_clover(values_real, values_imag, neighbours, gauge_links, back_links, clover):
    minus_real, minus_imag = projectors(-1.0)
    plus_real, plus_imag = projectors(1.0)
    summed_real, summed_imag = clover_apply(clover, values_real, values_imag)
    for direction in range(4):
        ahead_real, ahead_imag, behind_real, behind_imag = neighbours[direction]
        link_real = gauge_links[direction, :, :, 0].astype(jnp.float32)
        link_imag = gauge_links[direction, :, :, 1].astype(jnp.float32)
        step_real, step_imag = color_apply(link_real, link_imag, ahead_real, ahead_imag, False)
        step_real, step_imag = spin_apply(minus_real[direction], minus_imag[direction], step_real, step_imag)
        summed_real = summed_real - hopping * step_real
        summed_imag = summed_imag - hopping * step_imag
        link_real = back_links[direction, :, :, 0].astype(jnp.float32)
        link_imag = back_links[direction, :, :, 1].astype(jnp.float32)
        step_real, step_imag = color_apply(link_real, link_imag, behind_real, behind_imag, True)
        step_real, step_imag = spin_apply(plus_real[direction], plus_imag[direction], step_real, step_imag)
        summed_real = summed_real - hopping * step_real
        summed_imag = summed_imag - hopping * step_imag
    return (summed_real, summed_imag)

def shifted(values, site_axis, offset):
    if site_axis == 3:
        extent = values.shape[site_axis]
        blank_slab = jnp.zeros_like(lax.slice_in_dim(values, 0, 1, axis=site_axis))
        if offset > 0:
            return jnp.concatenate([lax.slice_in_dim(values, 1, extent, axis=site_axis), blank_slab], axis=site_axis)
        return jnp.concatenate([blank_slab, lax.slice_in_dim(values, 0, extent - 1, axis=site_axis)], axis=site_axis)
    return jnp.roll(values, -offset, axis=site_axis)

def reference(eigenvectors, gauge_links, back_links, clover, source_eigen, source_spin, source_parity):
    eigenvectors = eigenvectors.reshape(NT, NEV, 3, 2, NZ, NY, NX)
    gauge_links = gauge_links.reshape(4, 3, 3, 2, NT, NZ, NY, NX)
    back_links = back_links.reshape(4, 3, 3, 2, NT, NZ, NY, NX)
    clover = clover.reshape(2, 6, 6, 2, NT, NZ, NY, NX)
    grid_shape = (NT, NZ, NY, NX)
    parity = (lax.broadcasted_iota(jnp.int32, grid_shape, 0) + lax.broadcasted_iota(jnp.int32, grid_shape, 1) + lax.broadcasted_iota(jnp.int32, grid_shape, 2) + lax.broadcasted_iota(jnp.int32, grid_shape, 3)) % 2
    spin_grid = jnp.arange(4, dtype=jnp.int32)

    def one_source(source_index):
        chosen = lax.dynamic_index_in_dim(eigenvectors, source_eigen[source_index].astype(jnp.int32), 1, keepdims=False)
        chosen = jnp.transpose(chosen, (1, 2, 0, 3, 4, 5)).astype(jnp.float32)
        parity_keep = (parity == source_parity[source_index]).astype(jnp.float32)
        spin_pick = (spin_grid == source_spin[source_index]).astype(jnp.float32)[:, None, None, None, None, None]
        source_real = (spin_pick * (chosen[:, 0] * parity_keep)[None])[None]
        source_imag = (spin_pick * (chosen[:, 1] * parity_keep)[None])[None]
        neighbours = []
        for direction in range(4):
            site_axis = 6 - direction
            neighbours.append((shifted(source_real, site_axis, 1), shifted(source_imag, site_axis, 1), shifted(source_real, site_axis, -1), shifted(source_imag, site_axis, -1)))
        result_real, result_imag = wilson_clover(source_real, source_imag, neighbours, gauge_links, back_links, clover)
        return jnp.stack([result_real[0], result_imag[0]], axis=2).astype(jnp.bfloat16)
    propagated = lax.map(one_source, jnp.arange(NSRC, dtype=jnp.int32))
    norm_factor = 1.0 / math.sqrt(3.0 * NX * NY * NZ)

    def one_time(time_index):
        vectors = lax.dynamic_index_in_dim(eigenvectors, time_index, 0, keepdims=False).astype(jnp.float32)
        fields = lax.dynamic_index_in_dim(propagated, time_index, 4, keepdims=False).astype(jnp.float32)
        contraction = 'eczyx,baczyx->eab'
        highest = lax.Precision.HIGHEST
        real_sum = jnp.einsum(contraction, vectors[:, :, 0], fields[:, :, :, 0], precision=highest) + jnp.einsum(contraction, vectors[:, :, 1], fields[:, :, :, 1], precision=highest)
        imag_sum = jnp.einsum(contraction, vectors[:, :, 0], fields[:, :, :, 1], precision=highest) - jnp.einsum(contraction, vectors[:, :, 1], fields[:, :, :, 0], precision=highest)
        return jnp.stack([real_sum, imag_sum]).reshape(2, NEV, 4 * NSRC) * norm_factor
    projection = jnp.transpose(lax.map(one_time, jnp.arange(NT, dtype=jnp.int32)), (1, 0, 2, 3))
    return (propagated.reshape(NSRC, 4, 3, 2, NT, NZ, NY * NX), projection)
```

```python
import math

import jax
import jax.numpy as jnp
from jax import lax
from jax.experimental import pallas as pl
from jax.experimental.pallas import tpu as pltpu
from jax.sharding import Mesh, PartitionSpec as P

hopping = 0.125
SOURCES = 32
EIGEN = 128
SITES = 128
BLOCK = 16


def stencil_kernel(
    vectors_ref,
    center_ref,
    z_up_ref,
    z_down_ref,
    y_up_ref,
    y_down_ref,
    t_up_ref,
    t_down_ref,
    links_ref,
    back_ref,
    clover_ref,
    spin_ref,
    phase_ref,
    out_ref,
    sums_ref,
    rows_ref,
    fields_ref,
    links_f_ref,
    back_f_ref,
    clover_f_ref,
):
    links_f_ref[...] = links_ref[...].astype(jnp.float32)
    back_f_ref[...] = back_ref[...].astype(jnp.float32)
    clover_f_ref[...] = clover_ref[...].astype(jnp.float32)
    lane = lax.broadcasted_iota(jnp.int32, (BLOCK, SITES), 1)
    cell = lane & 63
    first_row = lane < 64
    last_cell = cell == 63
    first_cell = cell == 0
    site_parity = (lane + (lane >> 6)) & 1

    def link(ref, direction, row, column, part):
        index = ((direction * 3 + row) * 3 + column) * 2 + part
        return ref[pl.ds(index, 1), :]

    def forward(direction, real, imag):
        out = []
        for row in range(3):
            re = im = None
            for column in range(3):
                ur = link(links_f_ref, direction, row, column, 0)
                ui = link(links_f_ref, direction, row, column, 1)
                a = ur * real[column] - ui * imag[column]
                b = ur * imag[column] + ui * real[column]
                re = a if re is None else re + a
                im = b if im is None else im + b
            out.append((re, im))
        return out

    def backward(direction, real, imag):
        out = []
        for row in range(3):
            re = im = None
            for column in range(3):
                ur = link(back_f_ref, direction, column, row, 0)
                ui = link(back_f_ref, direction, column, row, 1)
                a = ur * real[column] + ui * imag[column]
                b = ur * imag[column] - ui * real[column]
                re = a if re is None else re + a
                im = b if im is None else im + b
            out.append((re, im))
        return out

    for start in range(0, SOURCES, BLOCK):
        block = pl.ds(start, BLOCK)
        spin = spin_ref[block, :]
        odd = (spin & 1) == 1
        high = spin >= 2
        match = phase_ref[block, :] == site_parity
        sign_x = jnp.where(high, 1.0, -1.0)
        sign_y = jnp.where(odd == high, -1.0, 1.0)

        def load(ref):
            return [ref[k, block, :].astype(jnp.float32) for k in range(6)]

        def both(direction, ahead, behind):
            fwd = forward(direction, ahead[0::2], ahead[1::2])
            bwd = backward(direction, behind[0::2], behind[1::2])
            plus = [(f[0] + b[0], f[1] + b[1]) for f, b in zip(fwd, bwd)]
            minus = [(b[0] - f[0], b[1] - f[1]) for f, b in zip(fwd, bwd)]
            return plus, minus

        center = load(center_ref)
        ahead = [jnp.where(last_cell, pltpu.roll(v, 63, 1), pltpu.roll(v, 127, 1)) for v in center]
        behind = [jnp.where(first_cell, pltpu.roll(v, 65, 1), pltpu.roll(v, 1, 1)) for v in center]
        total, minus = both(0, ahead, behind)
        cross = [(-sign_x * m[1], sign_x * m[0]) for m in minus]
        ahead = [
            pltpu.roll(jnp.where(first_row, n, v), 64, 1) for n, v in zip(load(y_up_ref), center)
        ]
        behind = [
            pltpu.roll(jnp.where(first_row, v, n), 64, 1) for n, v in zip(load(y_down_ref), center)
        ]
        plus, minus = both(1, ahead, behind)
        total = [(s[0] + p[0], s[1] + p[1]) for s, p in zip(total, plus)]
        cross = [(s[0] + sign_y * m[0], s[1] + sign_y * m[1]) for s, m in zip(cross, minus)]
        plus, minus = both(2, load(z_up_ref), load(z_down_ref))
        total = [(s[0] + p[0], s[1] + p[1]) for s, p in zip(total, plus)]
        along = [(-sign_y * m[1], sign_y * m[0]) for m in minus]
        plus, minus = both(3, load(t_up_ref), load(t_down_ref))
        total = [(s[0] + p[0], s[1] + p[1]) for s, p in zip(total, plus)]
        along = [(s[0] + m[0], s[1] + m[1]) for s, m in zip(along, minus)]

        def clover(block_index, row, column, part):
            index = ((block_index * 6 + row) * 6 + column) * 2 + part
            return clover_f_ref[pl.ds(index, 1), :]

        def clover_of(same, row, column, part):
            def one(half, low):
                line = 3 * low + row if same else 3 * (1 - low) + row
                return clover(half, line, 3 * low + column, part)

            lower = jnp.where(odd, one(0, 1), one(0, 0))
            upper = jnp.where(odd, one(1, 1), one(1, 0))
            return jnp.where(high, upper, lower)

        relative = [[], [], [], []]
        for colour in range(3):
            for same in (True, False):
                re = im = None
                for column in range(3):
                    cr = clover_of(same, colour, column, 0)
                    ci = clover_of(same, colour, column, 1)
                    vr, vi = center[2 * column], center[2 * column + 1]
                    a = cr * vr - ci * vi
                    b = cr * vi + ci * vr
                    re = a if re is None else re + a
                    im = b if im is None else im + b
                if same:
                    re = jnp.where(match, center[2 * colour] + re, -hopping * total[colour][0])
                    im = jnp.where(match, center[2 * colour + 1] + im, -hopping * total[colour][1])
                    relative[0] += [re, im]
                else:
                    relative[1] += [jnp.where(match, re, 0.0), jnp.where(match, im, 0.0)]
            relative[2] += [jnp.where(match, 0.0, -hopping * v) for v in along[colour]]
            relative[3] += [jnp.where(match, 0.0, -hopping * v) for v in cross[colour]]
        for k in range(6):
            once = [jnp.where(odd, relative[m ^ 1][k], relative[m][k]) for m in range(4)]
            for b in range(4):
                value = jnp.where(high, once[b ^ 2], once[b])
                rows_ref[pl.ds(start * 24 + b * 6 + k, BLOCK, stride=24), :] = value
                rounded = value.astype(jnp.bfloat16)
                at = pl.ds(b * SOURCES + start, BLOCK)
                fields_ref[at, pl.ds(k * SITES, SITES)] = rounded
                at = pl.ds((4 + b) * SOURCES + start, BLOCK)
                turned = rounded if k % 2 else -rounded
                fields_ref[at, pl.ds((k ^ 1) * SITES, SITES)] = turned
    out_ref[...] = rows_ref[...].astype(jnp.bfloat16)
    product = lax.dot_general(
        vectors_ref[...],
        fields_ref[...],
        (((1,), (1,)), ((), ())),
        preferred_element_type=jnp.float32,
    )
    sums_ref[0] = product[:, : 4 * SOURCES]
    sums_ref[1] = product[:, 4 * SOURCES :]


def apply_stencil(vectors, center, halos, links, back, clover, spin, phase):
    f32 = jnp.float32
    return pl.pallas_call(
        stencil_kernel,
        out_shape=(
            jax.ShapeDtypeStruct((SOURCES * 24, SITES), jnp.bfloat16),
            jax.ShapeDtypeStruct((2, EIGEN, 4 * SOURCES), f32),
        ),
        scratch_shapes=[
            pltpu.VMEM((SOURCES * 24, SITES), f32),
            pltpu.VMEM((8 * SOURCES, 6 * SITES), jnp.bfloat16),
            pltpu.VMEM((72, SITES), f32),
            pltpu.VMEM((72, SITES), f32),
            pltpu.VMEM((144, SITES), f32),
        ],
        compiler_params=pltpu.CompilerParams(vmem_limit_bytes=16 * 2**20),
        cost_estimate=pl.CostEstimate(
            flops=60_000_000, bytes_accessed=1_200_000, transcendentals=0
        ),
        name="stencil",
    )(vectors, center, *halos, links, back, clover, spin, phase)


DOMAIN = ("x", "y", "core")


def ring(count, step, closed=True):
    return [(i, (i + step) % count) for i in range(count) if closed or 0 <= i + step < count]


def body(eigenvectors, gauge_links, back_links, clover, source_eigen, source_spin, source_parity):
    pieces = eigenvectors.reshape(6, 16, 8, SITES).transpose(1, 2, 0, 3).reshape(4, 32, 6, SITES)
    arrived = lax.all_to_all(pieces, "zh", split_axis=0, concat_axis=0, tiled=True)
    arrived = lax.all_to_all(
        arrived.transpose(1, 0, 2, 3), DOMAIN, split_axis=0, concat_axis=0, tiled=True
    )
    vectors = arrived.transpose(1, 0, 2, 3).reshape(EIGEN, 6 * SITES)
    pick = source_eigen[:, None] == jnp.arange(EIGEN, dtype=jnp.int32)[None]
    center = jnp.dot(
        pick.astype(jnp.bfloat16), vectors, preferred_element_type=jnp.float32
    ).astype(jnp.bfloat16)
    center = center.reshape(SOURCES, 6, SITES).transpose(1, 0, 2)
    halos = [
        lax.ppermute(center, ("zh", "x"), ring(16, -1)),
        lax.ppermute(center, ("zh", "x"), ring(16, 1)),
        lax.ppermute(center, ("y", "core"), ring(8, -1)),
        lax.ppermute(center, ("y", "core"), ring(8, 1)),
        lax.ppermute(center, "ta", ring(4, -1, False)),
        lax.ppermute(center, "ta", ring(4, 1, False)),
    ]
    offset = lax.axis_index("ta") + lax.axis_index("x")
    spin = jnp.broadcast_to(source_spin[:, None], (SOURCES, SITES))
    phase = jnp.broadcast_to(((source_parity + offset) & 1)[:, None], (SOURCES, SITES))
    propagated, sums = apply_stencil(
        vectors,
        center,
        halos,
        gauge_links.reshape(72, SITES),
        back_links.reshape(72, SITES),
        clover.reshape(144, SITES),
        spin,
        phase,
    )
    parts = lax.all_to_all(sums.reshape(32, 8, 128), DOMAIN, split_axis=0, concat_axis=0, tiled=True)
    part = jnp.sum(parts, axis=0)
    parts = lax.all_to_all(
        jnp.broadcast_to(part[None], (4, 8, 128)), "zh", split_axis=0, concat_axis=0, tiled=True
    )
    part = jnp.sum(parts, axis=0) * (1.0 / math.sqrt(3.0 * 64 * 16 * 16))
    whole = lax.all_to_all(
        jnp.broadcast_to(part[None], (32, 8, 128)), DOMAIN, split_axis=0, concat_axis=0, tiled=True
    )
    return (
        propagated.reshape(SOURCES, 4, 3, 2, 1, 1, SITES),
        whole.reshape(2, 1, EIGEN, 4 * SOURCES),
    )


def solution(mesh):
    split = Mesh(mesh.devices.reshape(4, 4, 4, 4, 2), ("ta", "zh", "x", "y", "core"))
    fields = P(None, None, None, None, "ta", ("zh", "x"), ("y", "core"))
    return jax.shard_map(
        body,
        mesh=split,
        in_specs=(P("ta", ("zh", "x", "y", "core")), fields, fields, fields, P(), P(), P()),
        out_specs=(fields, P(None, "ta")),
        check_vma=False,
    )
```

```python
import math

import jax
import jax.numpy as jnp
from jax import lax
from jax.experimental import pallas as pl
from jax.experimental.pallas import tpu as pltpu
from jax.sharding import Mesh, PartitionSpec as P

hopping = 0.125
SOURCES = 32
EIGEN = 128
SITES = 128
BLOCK = 16


def stencil_kernel(
    vectors_ref,
    center_ref,
    t_up_ref,
    t_down_ref,
    links_ref,
    back_ref,
    clover_ref,
    code_ref,
    out_ref,
    sums_ref,
    rows_ref,
    fields_ref,
    links_f_ref,
    back_f_ref,
    clover_f_ref,
):
    links_f_ref[...] = links_ref[...].astype(jnp.float32)
    back_f_ref[...] = back_ref[...].astype(jnp.float32)
    clover_f_ref[...] = clover_ref[...].astype(jnp.float32)
    lane = lax.broadcasted_iota(jnp.int32, (BLOCK, SITES), 1)
    cell = lane & 63
    first_row = lane < 64
    last_cell = cell == 63
    first_cell = cell == 0
    site_parity = (lane + (lane >> 6)) & 1

    def link(ref, direction, row, column, part):
        index = ((direction * 3 + row) * 3 + column) * 2 + part
        return ref[pl.ds(index, 1), :]

    def forward(direction, real, imag):
        out = []
        for row in range(3):
            re = im = None
            for column in range(3):
                ur = link(links_f_ref, direction, row, column, 0)
                ui = link(links_f_ref, direction, row, column, 1)
                a = ur * real[column] - ui * imag[column]
                b = ur * imag[column] + ui * real[column]
                re = a if re is None else re + a
                im = b if im is None else im + b
            out.append((re, im))
        return out

    def backward(direction, real, imag):
        out = []
        for row in range(3):
            re = im = None
            for column in range(3):
                ur = link(back_f_ref, direction, column, row, 0)
                ui = link(back_f_ref, direction, column, row, 1)
                a = ur * real[column] + ui * imag[column]
                b = ur * imag[column] - ui * real[column]
                re = a if re is None else re + a
                im = b if im is None else im + b
            out.append((re, im))
        return out

    for start in range(0, SOURCES, BLOCK):
        block = pl.ds(start, BLOCK)
        code = code_ref[block, :]
        spin = code >> 3
        above = (code & 2) != 0
        below = (code & 4) != 0
        odd = (spin & 1) == 1
        high = spin >= 2
        match = (code & 1) == site_parity
        sign_x = jnp.where(high, 1.0, -1.0)
        sign_y = jnp.where(odd == high, -1.0, 1.0)

        def load(ref, first=0):
            return [ref[first + k, block, :].astype(jnp.float32) for k in range(6)]

        def both(direction, ahead, behind):
            fwd = forward(direction, ahead[0::2], ahead[1::2])
            bwd = backward(direction, behind[0::2], behind[1::2])
            plus = [(f[0] + b[0], f[1] + b[1]) for f, b in zip(fwd, bwd)]
            minus = [(b[0] - f[0], b[1] - f[1]) for f, b in zip(fwd, bwd)]
            return plus, minus

        center = load(center_ref)
        ahead = [jnp.where(last_cell, pltpu.roll(v, 63, 1), pltpu.roll(v, 127, 1)) for v in center]
        behind = [jnp.where(first_cell, pltpu.roll(v, 65, 1), pltpu.roll(v, 1, 1)) for v in center]
        total, minus = both(0, ahead, behind)
        cross = [(-sign_x * m[1], sign_x * m[0]) for m in minus]
        beside = load(center_ref, 18)
        ahead = [pltpu.roll(jnp.where(first_row, n, v), 64, 1) for n, v in zip(beside, center)]
        behind = [pltpu.roll(jnp.where(first_row, v, n), 64, 1) for n, v in zip(beside, center)]
        plus, minus = both(1, ahead, behind)
        total = [(s[0] + p[0], s[1] + p[1]) for s, p in zip(total, plus)]
        cross = [(s[0] + sign_y * m[0], s[1] + sign_y * m[1]) for s, m in zip(cross, minus)]
        plus, minus = both(2, load(center_ref, 12), load(center_ref, 6))
        total = [(s[0] + p[0], s[1] + p[1]) for s, p in zip(total, plus)]
        along = [(-sign_y * m[1], sign_y * m[0]) for m in minus]
        ahead = [jnp.where(above, v, 0.0) for v in load(t_up_ref)]
        behind = [jnp.where(below, v, 0.0) for v in load(t_down_ref)]
        plus, minus = both(3, ahead, behind)
        total = [(s[0] + p[0], s[1] + p[1]) for s, p in zip(total, plus)]
        along = [(s[0] + m[0], s[1] + m[1]) for s, m in zip(along, minus)]

        def clover(block_index, row, column, part):
            index = ((block_index * 6 + row) * 6 + column) * 2 + part
            return clover_f_ref[pl.ds(index, 1), :]

        def clover_of(same, row, column, part):
            def one(half, low):
                line = 3 * low + row if same else 3 * (1 - low) + row
                return clover(half, line, 3 * low + column, part)

            lower = jnp.where(odd, one(0, 1), one(0, 0))
            upper = jnp.where(odd, one(1, 1), one(1, 0))
            return jnp.where(high, upper, lower)

        relative = [[], [], [], []]
        for colour in range(3):
            for same in (True, False):
                re = im = None
                for column in range(3):
                    cr = clover_of(same, colour, column, 0)
                    ci = clover_of(same, colour, column, 1)
                    vr, vi = center[2 * column], center[2 * column + 1]
                    a = cr * vr - ci * vi
                    b = cr * vi + ci * vr
                    re = a if re is None else re + a
                    im = b if im is None else im + b
                if same:
                    re = jnp.where(match, center[2 * colour] + re, -hopping * total[colour][0])
                    im = jnp.where(match, center[2 * colour + 1] + im, -hopping * total[colour][1])
                    relative[0] += [re, im]
                else:
                    relative[1] += [jnp.where(match, re, 0.0), jnp.where(match, im, 0.0)]
            relative[2] += [jnp.where(match, 0.0, -hopping * v) for v in along[colour]]
            relative[3] += [jnp.where(match, 0.0, -hopping * v) for v in cross[colour]]
        for k in range(6):
            once = [jnp.where(odd, relative[m ^ 1][k], relative[m][k]) for m in range(4)]
            for b in range(4):
                value = jnp.where(high, once[b ^ 2], once[b])
                rows_ref[pl.ds(start * 24 + b * 6 + k, BLOCK, stride=24), :] = value
                rounded = value.astype(jnp.bfloat16)
                at = pl.ds(b * SOURCES + start, BLOCK)
                fields_ref[at, pl.ds(k * SITES, SITES)] = rounded
                at = pl.ds((4 + b) * SOURCES + start, BLOCK)
                turned = rounded if k % 2 else -rounded
                fields_ref[at, pl.ds((k ^ 1) * SITES, SITES)] = turned
    out_ref[...] = rows_ref[...].astype(jnp.bfloat16)
    product = lax.dot_general(
        vectors_ref[:, : 6 * SITES],
        fields_ref[...],
        (((1,), (1,)), ((), ())),
        preferred_element_type=jnp.float32,
    )
    sums_ref[0] = product[:, : 4 * SOURCES]
    sums_ref[1] = product[:, 4 * SOURCES :]


def apply_stencil(vectors, center, halos, links, back, clover, code):
    f32 = jnp.float32
    return pl.pallas_call(
        stencil_kernel,
        out_shape=(
            jax.ShapeDtypeStruct((SOURCES * 24, SITES), jnp.bfloat16),
            jax.ShapeDtypeStruct((2, EIGEN, 4 * SOURCES), f32),
        ),
        scratch_shapes=[
            pltpu.VMEM((SOURCES * 24, SITES), f32),
            pltpu.VMEM((8 * SOURCES, 6 * SITES), jnp.bfloat16),
            pltpu.VMEM((72, SITES), f32),
            pltpu.VMEM((72, SITES), f32),
            pltpu.VMEM((144, SITES), f32),
        ],
        compiler_params=pltpu.CompilerParams(vmem_limit_bytes=16 * 2**20),
        cost_estimate=pl.CostEstimate(
            flops=60_000_000, bytes_accessed=1_200_000, transcendentals=0
        ),
        name="stencil",
    )(vectors, center, *halos, links, back, clover, code)


DOMAIN = ("x", "y", "core")


def ring(count, step, closed=True):
    return [(i, (i + step) % count) for i in range(count) if closed or 0 <= i + step < count]


def body(eigenvectors, gauge_links, back_links, clover, source_eigen, source_spin, source_parity):
    cells = eigenvectors.reshape(6, 16, 8, SITES).transpose(1, 0, 2, 3)
    slabs = jnp.stack(
        [jnp.concatenate([cells[(4 * h - 1) % 16][None], cells[4 * h : 4 * h + 4], cells[(4 * h + 4) % 16][None]]) for h in range(4)]
    )
    slabs = lax.all_to_all(slabs, "zh", split_axis=0, concat_axis=0, tiled=True)
    own = slabs[:, 1:5]
    first_row = jnp.arange(SITES) < 64
    beside = jnp.where(first_row, jnp.roll(own, -1, axis=3), jnp.roll(own, 1, axis=3))
    pieces = jnp.stack([own, slabs[:, :4], slabs[:, 2:], beside])
    pieces = pieces.transpose(2, 4, 1, 0, 3, 5).reshape(32, 4, 24 * SITES)
    pieces = lax.all_to_all(pieces, DOMAIN, split_axis=0, concat_axis=0, tiled=True)
    vectors = pieces.reshape(EIGEN, 24 * SITES)
    row_of = (source_eigen % 32) * 4 + source_eigen // 32
    pick = row_of[:, None] == jnp.arange(EIGEN, dtype=jnp.int32)[None]
    center = jnp.dot(
        pick.astype(jnp.bfloat16), vectors, preferred_element_type=jnp.float32
    ).astype(jnp.bfloat16)
    center = center.reshape(SOURCES, 24, SITES).transpose(1, 0, 2)
    halos = [
        lax.ppermute(center[:6], "ta", ring(4, -1, False)),
        lax.ppermute(center[:6], "ta", ring(4, 1, False)),
    ]
    time = lax.axis_index("ta")
    code = (source_parity + time + lax.axis_index("x")) & 1
    code = code + 2 * (time < 3) + 4 * (time > 0) + 8 * source_spin
    code = jnp.broadcast_to(code[:, None], (SOURCES, SITES)).astype(jnp.int32)
    propagated, sums = apply_stencil(
        vectors,
        center,
        halos,
        gauge_links.reshape(72, SITES),
        back_links.reshape(72, SITES),
        clover.reshape(144, SITES),
        code,
    )
    sums = sums.reshape(2, 32, 4, 128).transpose(0, 2, 1, 3)
    parts = lax.all_to_all(sums.reshape(32, 8, 128), DOMAIN, split_axis=0, concat_axis=0, tiled=True)
    part = jnp.sum(parts, axis=0)
    parts = lax.all_to_all(
        jnp.broadcast_to(part[None], (4, 8, 128)), "zh", split_axis=0, concat_axis=0, tiled=True
    )
    part = jnp.sum(parts, axis=0) * (1.0 / math.sqrt(3.0 * 64 * 16 * 16))
    whole = lax.all_to_all(
        jnp.broadcast_to(part[None], (32, 8, 128)), DOMAIN, split_axis=0, concat_axis=0, tiled=True
    )
    return (
        propagated.reshape(SOURCES, 4, 3, 2, 1, 1, SITES),
        whole.reshape(2, 1, EIGEN, 4 * SOURCES),
    )


def solution(mesh):
    split = Mesh(mesh.devices.reshape(4, 4, 4, 4, 2), ("ta", "zh", "x", "y", "core"))
    fields = P(None, None, None, None, "ta", ("zh", "x"), ("y", "core"))
    return jax.shard_map(
        body,
        mesh=split,
        in_specs=(P("ta", ("zh", "x", "y", "core")), fields, fields, fields, P(), P(), P()),
        out_specs=(fields, P(None, "ta")),
        check_vma=False,
    )
```

```python
import math

import jax
import jax.numpy as jnp
from jax import lax
from jax.experimental import pallas as pl
from jax.experimental.pallas import tpu as pltpu
from jax.sharding import Mesh, PartitionSpec as P

hopping = 0.125
SOURCES = 32
EIGEN = 128
SITES = 128
BLOCK = 16


def chosen(pick_ref, vectors_ref, k):
    return jnp.dot(pick_ref[...], vectors_ref[k], preferred_element_type=jnp.float32)


def pick_kernel(pick_ref, vectors_ref, center_ref):
    for k in range(6):
        center_ref[k] = chosen(pick_ref, vectors_ref, k).astype(jnp.bfloat16)


def stencil_kernel(
    vectors_ref,
    pick_ref,
    center_ref,
    y_up_ref,
    y_down_ref,
    t_up_ref,
    t_down_ref,
    links_ref,
    back_ref,
    clover_ref,
    code_ref,
    out_ref,
    sums_ref,
    rows_ref,
    fields_ref,
    links_f_ref,
    back_f_ref,
    clover_f_ref,
    beside_ref,
):
    for k in range(12):
        beside_ref[k] = chosen(pick_ref, vectors_ref, 6 + k)
    links_f_ref[...] = links_ref[...].astype(jnp.float32)
    back_f_ref[...] = back_ref[...].astype(jnp.float32)
    clover_f_ref[...] = clover_ref[...].astype(jnp.float32)
    lane = lax.broadcasted_iota(jnp.int32, (BLOCK, SITES), 1)
    cell = lane & 63
    first_row = lane < 64
    last_cell = cell == 63
    first_cell = cell == 0
    site_parity = (lane + (lane >> 6)) & 1

    def link(ref, direction, row, column, part):
        index = ((direction * 3 + row) * 3 + column) * 2 + part
        return ref[pl.ds(index, 1), :]

    def forward(direction, real, imag):
        out = []
        for row in range(3):
            re = im = None
            for column in range(3):
                ur = link(links_f_ref, direction, row, column, 0)
                ui = link(links_f_ref, direction, row, column, 1)
                a = ur * real[column] - ui * imag[column]
                b = ur * imag[column] + ui * real[column]
                re = a if re is None else re + a
                im = b if im is None else im + b
            out.append((re, im))
        return out

    def backward(direction, real, imag):
        out = []
        for row in range(3):
            re = im = None
            for column in range(3):
                ur = link(back_f_ref, direction, column, row, 0)
                ui = link(back_f_ref, direction, column, row, 1)
                a = ur * real[column] + ui * imag[column]
                b = ur * imag[column] - ui * real[column]
                re = a if re is None else re + a
                im = b if im is None else im + b
            out.append((re, im))
        return out

    for start in range(0, SOURCES, BLOCK):
        block = pl.ds(start, BLOCK)
        code = code_ref[block, :]
        spin = code >> 3
        above = (code & 2) != 0
        below = (code & 4) != 0
        odd = (spin & 1) == 1
        high = spin >= 2
        match = (code & 1) == site_parity
        sign_x = jnp.where(high, 1.0, -1.0)
        sign_y = jnp.where(odd == high, -1.0, 1.0)

        def load(ref, first=0):
            return [ref[first + k, block, :].astype(jnp.float32) for k in range(6)]

        def both(direction, ahead, behind):
            fwd = forward(direction, ahead[0::2], ahead[1::2])
            bwd = backward(direction, behind[0::2], behind[1::2])
            plus = [(f[0] + b[0], f[1] + b[1]) for f, b in zip(fwd, bwd)]
            minus = [(b[0] - f[0], b[1] - f[1]) for f, b in zip(fwd, bwd)]
            return plus, minus

        center = load(center_ref)
        ahead = [jnp.where(last_cell, pltpu.roll(v, 63, 1), pltpu.roll(v, 127, 1)) for v in center]
        behind = [jnp.where(first_cell, pltpu.roll(v, 65, 1), pltpu.roll(v, 1, 1)) for v in center]
        total, minus = both(0, ahead, behind)
        cross = [(-sign_x * m[1], sign_x * m[0]) for m in minus]
        ahead = [
            pltpu.roll(jnp.where(first_row, n, v), 64, 1) for n, v in zip(load(y_up_ref), center)
        ]
        behind = [
            pltpu.roll(jnp.where(first_row, v, n), 64, 1) for n, v in zip(load(y_down_ref), center)
        ]
        plus, minus = both(1, ahead, behind)
        total = [(s[0] + p[0], s[1] + p[1]) for s, p in zip(total, plus)]
        cross = [(s[0] + sign_y * m[0], s[1] + sign_y * m[1]) for s, m in zip(cross, minus)]
        plus, minus = both(2, load(beside_ref, 6), load(beside_ref))
        total = [(s[0] + p[0], s[1] + p[1]) for s, p in zip(total, plus)]
        along = [(-sign_y * m[1], sign_y * m[0]) for m in minus]
        ahead = [jnp.where(above, v, 0.0) for v in load(t_up_ref)]
        behind = [jnp.where(below, v, 0.0) for v in load(t_down_ref)]
        plus, minus = both(3, ahead, behind)
        total = [(s[0] + p[0], s[1] + p[1]) for s, p in zip(total, plus)]
        along = [(s[0] + m[0], s[1] + m[1]) for s, m in zip(along, minus)]

        def clover(block_index, row, column, part):
            index = ((block_index * 6 + row) * 6 + column) * 2 + part
            return clover_f_ref[pl.ds(index, 1), :]

        def clover_of(same, row, column, part):
            def one(half, low):
                line = 3 * low + row if same else 3 * (1 - low) + row
                return clover(half, line, 3 * low + column, part)

            lower = jnp.where(odd, one(0, 1), one(0, 0))
            upper = jnp.where(odd, one(1, 1), one(1, 0))
            return jnp.where(high, upper, lower)

        relative = [[], [], [], []]
        for colour in range(3):
            for same in (True, False):
                re = im = None
                for column in range(3):
                    cr = clover_of(same, colour, column, 0)
                    ci = clover_of(same, colour, column, 1)
                    vr, vi = center[2 * column], center[2 * column + 1]
                    a = cr * vr - ci * vi
                    b = cr * vi + ci * vr
                    re = a if re is None else re + a
                    im = b if im is None else im + b
                if same:
                    re = jnp.where(match, center[2 * colour] + re, -hopping * total[colour][0])
                    im = jnp.where(match, center[2 * colour + 1] + im, -hopping * total[colour][1])
                    relative[0] += [re, im]
                else:
                    relative[1] += [jnp.where(match, re, 0.0), jnp.where(match, im, 0.0)]
            relative[2] += [jnp.where(match, 0.0, -hopping * v) for v in along[colour]]
            relative[3] += [jnp.where(match, 0.0, -hopping * v) for v in cross[colour]]
        for k in range(6):
            once = [jnp.where(odd, relative[m ^ 1][k], relative[m][k]) for m in range(4)]
            for b in range(4):
                value = jnp.where(high, once[b ^ 2], once[b])
                rows_ref[pl.ds(start * 24 + b * 6 + k, BLOCK, stride=24), :] = value
                rounded = value.astype(jnp.bfloat16)
                at = pl.ds(b * SOURCES + start, BLOCK)
                fields_ref[at, pl.ds(k * SITES, SITES)] = rounded
                at = pl.ds((4 + b) * SOURCES + start, BLOCK)
                turned = rounded if k % 2 else -rounded
                fields_ref[at, pl.ds((k ^ 1) * SITES, SITES)] = turned
    out_ref[...] = rows_ref[...].astype(jnp.bfloat16)
    product = None
    for k in range(6):
        term = lax.dot_general(
            vectors_ref[k],
            fields_ref[:, pl.ds(k * SITES, SITES)],
            (((1,), (1,)), ((), ())),
            preferred_element_type=jnp.float32,
        )
        product = term if product is None else product + term
    sums_ref[0] = product[:, : 4 * SOURCES]
    sums_ref[1] = product[:, 4 * SOURCES :]


def pick_sources(pick, vectors):
    return pl.pallas_call(
        pick_kernel,
        grid=(1,),
        in_specs=[
            pl.BlockSpec((SOURCES, EIGEN), lambda i: (0, 0)),
            pl.BlockSpec((6, EIGEN, SITES), lambda i: (0, 0, 0)),
        ],
        out_specs=pl.BlockSpec((6, SOURCES, SITES), lambda i: (0, 0, 0)),
        out_shape=jax.ShapeDtypeStruct((6, SOURCES, SITES), jnp.bfloat16),
        compiler_params=pltpu.CompilerParams(vmem_limit_bytes=8 * 2**20),
        name="pick",
    )(pick, vectors)


def apply_stencil(vectors, pick, center, halos, links, back, clover, code):
    f32 = jnp.float32
    return pl.pallas_call(
        stencil_kernel,
        out_shape=(
            jax.ShapeDtypeStruct((SOURCES * 24, SITES), jnp.bfloat16),
            jax.ShapeDtypeStruct((2, EIGEN, 4 * SOURCES), f32),
        ),
        scratch_shapes=[
            pltpu.VMEM((SOURCES * 24, SITES), f32),
            pltpu.VMEM((8 * SOURCES, 6 * SITES), jnp.bfloat16),
            pltpu.VMEM((72, SITES), f32),
            pltpu.VMEM((72, SITES), f32),
            pltpu.VMEM((144, SITES), f32),
            pltpu.VMEM((12, SOURCES, SITES), f32),
        ],
        compiler_params=pltpu.CompilerParams(vmem_limit_bytes=16 * 2**20),
        cost_estimate=pl.CostEstimate(
            flops=60_000_000, bytes_accessed=1_200_000, transcendentals=0
        ),
        name="stencil",
    )(vectors, pick, center, *halos, links, back, clover, code)


DOMAIN = ("x", "y", "core")


def ring(count, step, closed=True):
    return [(i, (i + step) % count) for i in range(count) if closed or 0 <= i + step < count]


def body(eigenvectors, gauge_links, back_links, clover, source_eigen, source_spin, source_parity):
    time = lax.axis_index("ta")
    code = (source_parity + time + lax.axis_index("x")) & 1
    code = code + 2 * (time < 3) + 4 * (time > 0) + 8 * source_spin
    code = jnp.broadcast_to(code[:, None], (SOURCES, SITES)).astype(jnp.int32)
    row_of = (source_eigen % 32) * 4 + source_eigen // 32
    pick = row_of[:, None] == jnp.arange(EIGEN, dtype=jnp.int32)[None]
    pick = pick.astype(jnp.bfloat16)
    links, back, clover = (
        gauge_links.reshape(72, SITES),
        back_links.reshape(72, SITES),
        clover.reshape(144, SITES),
    )
    cells = eigenvectors.reshape(6, 16, 8, SITES).transpose(1, 0, 2, 3)
    slabs = jnp.stack(
        [
            jnp.concatenate(
                [cells[(4 * h - 1) % 16][None], cells[4 * h : 4 * h + 4], cells[(4 * h + 4) % 16][None]]
            )
            for h in range(4)
        ]
    )
    slabs = lax.all_to_all(slabs, "zh", split_axis=0, concat_axis=0, tiled=True)
    slabs = slabs.transpose(1, 3, 2, 0, 4).reshape(6, 8, 24, SITES)
    pieces = jnp.stack([slabs[1:5], slabs[:4], slabs[2:]], axis=2).reshape(32, 72, SITES)
    pieces = lax.all_to_all(pieces, DOMAIN, split_axis=0, concat_axis=0, tiled=True)
    vectors = pieces.reshape(32, 18, 4, SITES).transpose(1, 0, 2, 3).reshape(18, EIGEN, SITES)
    center = pick_sources(pick, vectors)
    halos = [
        lax.ppermute(center, ("y", "core"), ring(8, -1)),
        lax.ppermute(center, ("y", "core"), ring(8, 1)),
        lax.ppermute(center, "ta", ring(4, -1, False)),
        lax.ppermute(center, "ta", ring(4, 1, False)),
    ]
    propagated, sums = apply_stencil(vectors, pick, center, halos, links, back, clover, code)
    sums = sums.reshape(2, 32, 4, 128).transpose(0, 2, 1, 3)
    parts = lax.all_to_all(sums.reshape(32, 8, 128), DOMAIN, split_axis=0, concat_axis=0, tiled=True)
    part = jnp.sum(parts, axis=0)
    parts = lax.all_to_all(
        jnp.broadcast_to(part[None], (4, 8, 128)), "zh", split_axis=0, concat_axis=0, tiled=True
    )
    part = jnp.sum(parts, axis=0) * (1.0 / math.sqrt(3.0 * 64 * 16 * 16))
    whole = lax.all_to_all(
        jnp.broadcast_to(part[None], (32, 8, 128)), DOMAIN, split_axis=0, concat_axis=0, tiled=True
    )
    return (
        propagated.reshape(SOURCES, 4, 3, 2, 1, 1, SITES),
        whole.reshape(2, 1, EIGEN, 4 * SOURCES),
    )


def solution(mesh):
    split = Mesh(mesh.devices.reshape(4, 4, 4, 4, 2), ("ta", "zh", "x", "y", "core"))
    fields = P(None, None, None, None, "ta", ("zh", "x"), ("y", "core"))
    return jax.shard_map(
        body,
        mesh=split,
        in_specs=(P("ta", ("zh", "x", "y", "core")), fields, fields, fields, P(), P(), P()),
        out_specs=(fields, P(None, "ta")),
        check_vma=False,
    )
```

```python
import math

import jax
import jax.numpy as jnp
from jax import lax
from jax.experimental import pallas as pl
from jax.experimental.pallas import tpu as pltpu
from jax.sharding import Mesh, PartitionSpec as P

hopping = 0.125
SOURCES = 32
EIGEN = 128
SITES = 128
BLOCK = 16


def chosen(pick_ref, vectors_ref, k):
    return jnp.dot(pick_ref[...], vectors_ref[k], preferred_element_type=jnp.float32)


def pick_kernel(pick_ref, vectors_ref, code_ref, center_ref, halved_ref):
    lane = lax.broadcasted_iota(jnp.int32, (SOURCES, SITES), 1)
    match = (code_ref[...] & 1) == ((lane + (lane >> 6)) & 1)
    used = []
    for k in range(6):
        value = chosen(pick_ref, vectors_ref, k)
        center_ref[k] = value.astype(jnp.bfloat16)
        used.append(jnp.where(match, value, pltpu.roll(value, 64, 1)))
    for colour in range(3):
        halved_ref[colour] = jnp.where(lane < 64, used[2 * colour], used[2 * colour + 1]).astype(
            jnp.bfloat16
        )


def colour_forward(ref, direction, real, imag):
    out = []
    for row in range(3):
        re = im = None
        for column in range(3):
            index = ((direction * 3 + row) * 3 + column) * 2
            ur, ui = ref[pl.ds(index, 1), :], ref[pl.ds(index + 1, 1), :]
            a = ur * real[column] - ui * imag[column]
            b = ur * imag[column] + ui * real[column]
            re = a if re is None else re + a
            im = b if im is None else im + b
        out.append((re, im))
    return out


def colour_backward(ref, direction, real, imag):
    out = []
    for row in range(3):
        re = im = None
        for column in range(3):
            index = ((direction * 3 + column) * 3 + row) * 2
            ur, ui = ref[pl.ds(index, 1), :], ref[pl.ds(index + 1, 1), :]
            a = ur * real[column] + ui * imag[column]
            b = ur * imag[column] - ui * real[column]
            re = a if re is None else re + a
            im = b if im is None else im + b
        out.append((re, im))
    return out


def both(links_ref, back_ref, direction, ahead, behind):
    fwd = colour_forward(links_ref, direction, ahead[0::2], ahead[1::2])
    bwd = colour_backward(back_ref, direction, behind[0::2], behind[1::2])
    plus = [(f[0] + b[0], f[1] + b[1]) for f, b in zip(fwd, bwd)]
    minus = [(b[0] - f[0], b[1] - f[1]) for f, b in zip(fwd, bwd)]
    return plus, minus


def space_kernel(
    others_ref,
    pick_ref,
    center_ref,
    y_up_ref,
    y_down_ref,
    links_ref,
    back_ref,
    clover_ref,
    code_ref,
    base_ref,
    links_f_ref,
    back_f_ref,
    clover_f_ref,
    beside_ref,
):
    for k in range(12):
        beside_ref[k] = chosen(pick_ref, others_ref, k)
    links_f_ref[...] = links_ref[...].astype(jnp.float32)
    back_f_ref[...] = back_ref[...].astype(jnp.float32)
    clover_f_ref[...] = clover_ref[...].astype(jnp.float32)
    lane = lax.broadcasted_iota(jnp.int32, (BLOCK, SITES), 1)
    cell = lane & 63
    first_row = lane < 64
    last_cell = cell == 63
    first_cell = cell == 0
    site_parity = (lane + (lane >> 6)) & 1

    for start in range(0, SOURCES, BLOCK):
        block = pl.ds(start, BLOCK)
        code = code_ref[block, :]
        spin = code >> 3
        odd = (spin & 1) == 1
        high = spin >= 2
        match = (code & 1) == site_parity
        sign_x = jnp.where(high, 1.0, -1.0)
        sign_y = jnp.where(odd == high, -1.0, 1.0)

        def load(ref, first=0):
            return [ref[first + k, block, :].astype(jnp.float32) for k in range(6)]

        center = load(center_ref)
        ahead = [jnp.where(last_cell, pltpu.roll(v, 63, 1), pltpu.roll(v, 127, 1)) for v in center]
        behind = [jnp.where(first_cell, pltpu.roll(v, 65, 1), pltpu.roll(v, 1, 1)) for v in center]
        total, minus = both(links_f_ref, back_f_ref, 0, ahead, behind)
        cross = [(-sign_x * m[1], sign_x * m[0]) for m in minus]
        ahead = [
            pltpu.roll(jnp.where(first_row, n, v), 64, 1) for n, v in zip(load(y_up_ref), center)
        ]
        behind = [
            pltpu.roll(jnp.where(first_row, v, n), 64, 1) for n, v in zip(load(y_down_ref), center)
        ]
        plus, minus = both(links_f_ref, back_f_ref, 1, ahead, behind)
        total = [(s[0] + p[0], s[1] + p[1]) for s, p in zip(total, plus)]
        cross = [(s[0] + sign_y * m[0], s[1] + sign_y * m[1]) for s, m in zip(cross, minus)]
        plus, minus = both(links_f_ref, back_f_ref, 2, load(beside_ref, 6), load(beside_ref))
        total = [(s[0] + p[0], s[1] + p[1]) for s, p in zip(total, plus)]
        along = [(-sign_y * m[1], sign_y * m[0]) for m in minus]
        def clover(block_index, row, column, part):
            index = ((block_index * 6 + row) * 6 + column) * 2 + part
            return clover_f_ref[pl.ds(index, 1), :]

        def clover_of(same, row, column, part):
            def one(half, low):
                line = 3 * low + row if same else 3 * (1 - low) + row
                return clover(half, line, 3 * low + column, part)

            lower = jnp.where(odd, one(0, 1), one(0, 0))
            upper = jnp.where(odd, one(1, 1), one(1, 0))
            return jnp.where(high, upper, lower)

        relative = [[], [], [], []]
        for colour in range(3):
            for same in (True, False):
                re = im = None
                for column in range(3):
                    cr = clover_of(same, colour, column, 0)
                    ci = clover_of(same, colour, column, 1)
                    vr, vi = center[2 * column], center[2 * column + 1]
                    a = cr * vr - ci * vi
                    b = cr * vi + ci * vr
                    re = a if re is None else re + a
                    im = b if im is None else im + b
                if same:
                    re = jnp.where(match, center[2 * colour] + re, -hopping * total[colour][0])
                    im = jnp.where(match, center[2 * colour + 1] + im, -hopping * total[colour][1])
                    relative[0] += [re, im]
                else:
                    relative[1] += [jnp.where(match, re, 0.0), jnp.where(match, im, 0.0)]
            relative[2] += [jnp.where(match, 0.0, -hopping * v) for v in along[colour]]
            relative[3] += [jnp.where(match, 0.0, -hopping * v) for v in cross[colour]]
        for m in range(4):
            for k in range(6):
                base_ref[6 * m + k, block, :] = relative[m][k]


def spread(ref, block, there, first_row):
    out = []
    for colour in range(3):
        value = jnp.where(there, ref[colour, block, :].astype(jnp.float32), 0.0)
        turned = pltpu.roll(value, 64, 1)
        out += [jnp.where(first_row, value, turned), jnp.where(first_row, turned, value)]
    return out


def time_kernel(
    vectors_ref,
    base_ref,
    t_up_ref,
    t_down_ref,
    links_ref,
    back_ref,
    code_ref,
    out_ref,
    sums_ref,
    rows_ref,
    fields_ref,
    links_f_ref,
    back_f_ref,
):
    links_f_ref[...] = links_ref[...].astype(jnp.float32)
    back_f_ref[...] = back_ref[...].astype(jnp.float32)
    lane = lax.broadcasted_iota(jnp.int32, (BLOCK, SITES), 1)
    first_row = lane < 64
    site_parity = (lane + (lane >> 6)) & 1
    for start in range(0, SOURCES, BLOCK):
        block = pl.ds(start, BLOCK)
        code = code_ref[block, :]
        spin = code >> 3
        above = (code & 2) != 0
        below = (code & 4) != 0
        odd = (spin & 1) == 1
        high = spin >= 2
        match = (code & 1) == site_parity
        ahead = spread(t_up_ref, block, above, first_row)
        behind = spread(t_down_ref, block, below, first_row)
        plus, minus = both(links_f_ref, back_f_ref, 3, ahead, behind)
        relative = [[base_ref[6 * m + k, block, :] for k in range(6)] for m in range(4)]
        for colour in range(3):
            for part in range(2):
                k = 2 * colour + part
                relative[0][k] += jnp.where(match, 0.0, -hopping * plus[colour][part])
                relative[2][k] += jnp.where(match, 0.0, -hopping * minus[colour][part])
        for k in range(6):
            once = [jnp.where(odd, relative[m ^ 1][k], relative[m][k]) for m in range(4)]
            for b in range(4):
                value = jnp.where(high, once[b ^ 2], once[b])
                rows_ref[pl.ds(start * 24 + b * 6 + k, BLOCK, stride=24), :] = value
                rounded = value.astype(jnp.bfloat16)
                at = pl.ds(b * SOURCES + start, BLOCK)
                fields_ref[at, pl.ds(k * SITES, SITES)] = rounded
                at = pl.ds((4 + b) * SOURCES + start, BLOCK)
                turned = rounded if k % 2 else -rounded
                fields_ref[at, pl.ds((k ^ 1) * SITES, SITES)] = turned
    out_ref[...] = rows_ref[...].astype(jnp.bfloat16)
    product = None
    for k in range(6):
        term = lax.dot_general(
            vectors_ref[k],
            fields_ref[:, pl.ds(k * SITES, SITES)],
            (((1,), (1,)), ((), ())),
            preferred_element_type=jnp.float32,
        )
        product = term if product is None else product + term
    sums_ref[0] = product[:, : 4 * SOURCES]
    sums_ref[1] = product[:, 4 * SOURCES :]


def pick_sources(pick, vectors, code):
    return pl.pallas_call(
        pick_kernel,
        out_shape=(
            jax.ShapeDtypeStruct((6, SOURCES, SITES), jnp.bfloat16),
            jax.ShapeDtypeStruct((3, SOURCES, SITES), jnp.bfloat16),
        ),
        compiler_params=pltpu.CompilerParams(vmem_limit_bytes=8 * 2**20),
        name="pick",
    )(pick, vectors, code)


def space_part(others, pick, center, y_up, y_down, links, back, clover, code):
    f32 = jnp.float32
    return pl.pallas_call(
        space_kernel,
        out_shape=jax.ShapeDtypeStruct((24, SOURCES, SITES), f32),
        scratch_shapes=[
            pltpu.VMEM((72, SITES), f32),
            pltpu.VMEM((72, SITES), f32),
            pltpu.VMEM((144, SITES), f32),
            pltpu.VMEM((12, SOURCES, SITES), f32),
        ],
        compiler_params=pltpu.CompilerParams(vmem_limit_bytes=16 * 2**20),
        cost_estimate=pl.CostEstimate(
            flops=20_000_000, bytes_accessed=1_200_000, transcendentals=0
        ),
        name="space",
    )(others, pick, center, y_up, y_down, links, back, clover, code)


def time_part(vectors, base, t_up, t_down, links, back, code):
    f32 = jnp.float32
    return pl.pallas_call(
        time_kernel,
        out_shape=(
            jax.ShapeDtypeStruct((SOURCES * 24, SITES), jnp.bfloat16),
            jax.ShapeDtypeStruct((2, EIGEN, 4 * SOURCES), f32),
        ),
        scratch_shapes=[
            pltpu.VMEM((SOURCES * 24, SITES), f32),
            pltpu.VMEM((8 * SOURCES, 6 * SITES), jnp.bfloat16),
            pltpu.VMEM((72, SITES), f32),
            pltpu.VMEM((72, SITES), f32),
        ],
        compiler_params=pltpu.CompilerParams(vmem_limit_bytes=16 * 2**20),
        cost_estimate=pl.CostEstimate(
            flops=60_000_000, bytes_accessed=1_200_000, transcendentals=0
        ),
        name="time",
    )(vectors, base, t_up, t_down, links, back, code)


DOMAIN = ("x", "y", "core")


def ring(count, step, closed=True):
    return [(i, (i + step) % count) for i in range(count) if closed or 0 <= i + step < count]


def body(eigenvectors, gauge_links, back_links, clover, source_eigen, source_spin, source_parity):
    time = lax.axis_index("ta")
    offset = (time + lax.axis_index("x")) & 1
    ends = 2 * (time < 3).astype(jnp.int32) + 4 * (time > 0).astype(jnp.int32)
    eigenvectors, offset, ends = lax.optimization_barrier((eigenvectors, offset, ends))
    code = ((source_parity + offset) & 1) + ends + 8 * source_spin
    code = jnp.broadcast_to(code[:, None], (SOURCES, SITES)).astype(jnp.int32)
    row_of = (source_eigen % 32) * 4 + source_eigen // 32
    pick = row_of[:, None] == jnp.arange(EIGEN, dtype=jnp.int32)[None]
    pick = pick.astype(jnp.bfloat16)
    links, back, clover = (
        gauge_links.reshape(72, SITES),
        back_links.reshape(72, SITES),
        clover.reshape(144, SITES),
    )
    cells = eigenvectors.reshape(6, 16, 8, SITES).transpose(1, 0, 2, 3)
    slabs = jnp.stack(
        [
            jnp.concatenate(
                [cells[(4 * h - 1) % 16][None], cells[4 * h : 4 * h + 4], cells[(4 * h + 4) % 16][None]]
            )
            for h in range(4)
        ]
    )
    slabs = lax.all_to_all(slabs, "zh", split_axis=0, concat_axis=0, tiled=True)
    slabs = slabs.transpose(1, 3, 2, 0, 4).reshape(6, 8, 24, SITES)
    pieces = jnp.stack([slabs[1:5], slabs[:4], slabs[2:]], axis=2).reshape(32, 72, SITES)
    pieces = lax.all_to_all(pieces, DOMAIN, split_axis=0, concat_axis=0, tiled=True)
    pieces = pieces.reshape(32, 18, 4, SITES)
    vectors = pieces[:, :6].transpose(1, 0, 2, 3).reshape(6, EIGEN, SITES)
    others = pieces[:, 6:].transpose(1, 0, 2, 3).reshape(12, EIGEN, SITES)
    center, halved = pick_sources(pick, vectors, code)
    halos = [
        lax.ppermute(center, ("y", "core"), ring(8, -1)),
        lax.ppermute(center, ("y", "core"), ring(8, 1)),
        lax.ppermute(halved, "ta", ring(4, -1, False)),
        lax.ppermute(halved, "ta", ring(4, 1, False)),
    ]
    base = space_part(others, pick, center, halos[0], halos[1], links, back, clover, code)
    propagated, sums = time_part(vectors, base, halos[2], halos[3], links, back, code)
    sums = sums.reshape(2, 32, 4, 128).transpose(0, 2, 1, 3)
    parts = sums.reshape(8, 4, 8, 128).transpose(1, 0, 2, 3).reshape(32, 8, 128)
    parts = lax.all_to_all(parts, DOMAIN, split_axis=0, concat_axis=0, tiled=True)
    part = jnp.sum(parts, axis=0)
    parts = lax.all_to_all(
        jnp.broadcast_to(part[None], (16, 8, 128)), ("zh", "x"), split_axis=0, concat_axis=0, tiled=True
    )
    part = jnp.sum(parts.reshape(4, 32, 128), axis=0) * (1.0 / math.sqrt(3.0 * 64 * 16 * 16))
    whole = lax.all_to_all(
        jnp.broadcast_to(part[None], (8, 32, 128)), ("y", "core"), split_axis=0, concat_axis=0, tiled=True
    )
    return (
        propagated.reshape(SOURCES, 4, 3, 2, 1, 1, SITES),
        whole.reshape(2, 1, EIGEN, 4 * SOURCES),
    )


def solution(mesh):
    split = Mesh(mesh.devices.reshape(4, 4, 4, 4, 2), ("ta", "zh", "x", "y", "core"))
    fields = P(None, None, None, None, "ta", ("zh", "x"), ("y", "core"))
    return jax.shard_map(
        body,
        mesh=split,
        in_specs=(P("ta", ("zh", "x", "y", "core")), fields, fields, fields, P(), P(), P()),
        out_specs=(fields, P(None, "ta")),
        check_vma=False,
    )
```

```python
import math

import jax
import jax.numpy as jnp
from jax import lax
from jax.experimental import pallas as pl
from jax.experimental.pallas import tpu as pltpu
from jax.sharding import Mesh, PartitionSpec as P

hopping = 0.125
SOURCES = 32
EIGEN = 128
SITES = 128
BLOCK = 16


def chosen(pick_ref, vectors_ref, k):
    return jnp.dot(pick_ref[...], vectors_ref[k], preferred_element_type=jnp.float32)


def pick_kernel(pick_ref, vectors_ref, code_ref, center_ref, halved_ref):
    lane = lax.broadcasted_iota(jnp.int32, (SOURCES, SITES), 1)
    match = (code_ref[...] & 1) == ((lane + (lane >> 6)) & 1)
    used = []
    for k in range(6):
        value = chosen(pick_ref, vectors_ref, k)
        center_ref[k] = value.astype(jnp.bfloat16)
        used.append(jnp.where(match, value, pltpu.roll(value, 64, 1)))
    for colour in range(3):
        halved = jnp.where(lane < 64, used[2 * colour], used[2 * colour + 1]).astype(jnp.bfloat16)
        for slice_index in range(4):
            halved_ref[slice_index, colour] = halved


def colour_forward(ref, direction, real, imag):
    out = []
    for row in range(3):
        re = im = None
        for column in range(3):
            index = ((direction * 3 + row) * 3 + column) * 2
            ur, ui = ref[pl.ds(index, 1), :], ref[pl.ds(index + 1, 1), :]
            a = ur * real[column] - ui * imag[column]
            b = ur * imag[column] + ui * real[column]
            re = a if re is None else re + a
            im = b if im is None else im + b
        out.append((re, im))
    return out


def colour_backward(ref, direction, real, imag):
    out = []
    for row in range(3):
        re = im = None
        for column in range(3):
            index = ((direction * 3 + column) * 3 + row) * 2
            ur, ui = ref[pl.ds(index, 1), :], ref[pl.ds(index + 1, 1), :]
            a = ur * real[column] + ui * imag[column]
            b = ur * imag[column] - ui * real[column]
            re = a if re is None else re + a
            im = b if im is None else im + b
        out.append((re, im))
    return out


def both(links_ref, back_ref, direction, ahead, behind):
    fwd = colour_forward(links_ref, direction, ahead[0::2], ahead[1::2])
    bwd = colour_backward(back_ref, direction, behind[0::2], behind[1::2])
    plus = [(f[0] + b[0], f[1] + b[1]) for f, b in zip(fwd, bwd)]
    minus = [(b[0] - f[0], b[1] - f[1]) for f, b in zip(fwd, bwd)]
    return plus, minus


def space_kernel(
    others_ref,
    pick_ref,
    center_ref,
    y_up_ref,
    y_down_ref,
    links_ref,
    back_ref,
    clover_ref,
    code_ref,
    base_ref,
    links_f_ref,
    back_f_ref,
    clover_f_ref,
    beside_ref,
):
    for k in range(12):
        beside_ref[k] = chosen(pick_ref, others_ref, k)
    links_f_ref[...] = links_ref[...].astype(jnp.float32)
    back_f_ref[...] = back_ref[...].astype(jnp.float32)
    clover_f_ref[...] = clover_ref[...].astype(jnp.float32)
    lane = lax.broadcasted_iota(jnp.int32, (BLOCK, SITES), 1)
    cell = lane & 63
    first_row = lane < 64
    last_cell = cell == 63
    first_cell = cell == 0
    site_parity = (lane + (lane >> 6)) & 1

    for start in range(0, SOURCES, BLOCK):
        block = pl.ds(start, BLOCK)
        code = code_ref[block, :]
        spin = code >> 3
        odd = (spin & 1) == 1
        high = spin >= 2
        match = (code & 1) == site_parity
        sign_x = jnp.where(high, 1.0, -1.0)
        sign_y = jnp.where(odd == high, -1.0, 1.0)

        def load(ref, first=0):
            return [ref[first + k, block, :].astype(jnp.float32) for k in range(6)]

        center = load(center_ref)
        ahead = [jnp.where(last_cell, pltpu.roll(v, 63, 1), pltpu.roll(v, 127, 1)) for v in center]
        behind = [jnp.where(first_cell, pltpu.roll(v, 65, 1), pltpu.roll(v, 1, 1)) for v in center]
        total, minus = both(links_f_ref, back_f_ref, 0, ahead, behind)
        cross = [(-sign_x * m[1], sign_x * m[0]) for m in minus]
        ahead = [
            pltpu.roll(jnp.where(first_row, n, v), 64, 1) for n, v in zip(load(y_up_ref), center)
        ]
        behind = [
            pltpu.roll(jnp.where(first_row, v, n), 64, 1) for n, v in zip(load(y_down_ref), center)
        ]
        plus, minus = both(links_f_ref, back_f_ref, 1, ahead, behind)
        total = [(s[0] + p[0], s[1] + p[1]) for s, p in zip(total, plus)]
        cross = [(s[0] + sign_y * m[0], s[1] + sign_y * m[1]) for s, m in zip(cross, minus)]
        plus, minus = both(links_f_ref, back_f_ref, 2, load(beside_ref, 6), load(beside_ref))
        total = [(s[0] + p[0], s[1] + p[1]) for s, p in zip(total, plus)]
        along = [(-sign_y * m[1], sign_y * m[0]) for m in minus]
        def clover(block_index, row, column, part):
            index = ((block_index * 6 + row) * 6 + column) * 2 + part
            return clover_f_ref[pl.ds(index, 1), :]

        def clover_of(same, row, column, part):
            def one(half, low):
                line = 3 * low + row if same else 3 * (1 - low) + row
                return clover(half, line, 3 * low + column, part)

            lower = jnp.where(odd, one(0, 1), one(0, 0))
            upper = jnp.where(odd, one(1, 1), one(1, 0))
            return jnp.where(high, upper, lower)

        relative = [[], [], [], []]
        for colour in range(3):
            for same in (True, False):
                re = im = None
                for column in range(3):
                    cr = clover_of(same, colour, column, 0)
                    ci = clover_of(same, colour, column, 1)
                    vr, vi = center[2 * column], center[2 * column + 1]
                    a = cr * vr - ci * vi
                    b = cr * vi + ci * vr
                    re = a if re is None else re + a
                    im = b if im is None else im + b
                if same:
                    re = jnp.where(match, center[2 * colour] + re, -hopping * total[colour][0])
                    im = jnp.where(match, center[2 * colour + 1] + im, -hopping * total[colour][1])
                    relative[0] += [re, im]
                else:
                    relative[1] += [jnp.where(match, re, 0.0), jnp.where(match, im, 0.0)]
            relative[2] += [jnp.where(match, 0.0, -hopping * v) for v in along[colour]]
            relative[3] += [jnp.where(match, 0.0, -hopping * v) for v in cross[colour]]
        for m in range(4):
            for k in range(6):
                base_ref[6 * m + k, block, :] = relative[m][k]


def spread(ref, block, there, first_row):
    out = []
    for colour in range(3):
        value = jnp.where(there, ref[colour, block, :].astype(jnp.float32), 0.0)
        turned = pltpu.roll(value, 64, 1)
        out += [jnp.where(first_row, value, turned), jnp.where(first_row, turned, value)]
    return out


def time_kernel(
    vectors_ref,
    base_ref,
    t_up_ref,
    t_down_ref,
    links_ref,
    back_ref,
    code_ref,
    out_ref,
    sums_ref,
    rows_ref,
    fields_ref,
    links_f_ref,
    back_f_ref,
):
    links_f_ref[...] = links_ref[...].astype(jnp.float32)
    back_f_ref[...] = back_ref[...].astype(jnp.float32)
    lane = lax.broadcasted_iota(jnp.int32, (BLOCK, SITES), 1)
    first_row = lane < 64
    site_parity = (lane + (lane >> 6)) & 1
    for start in range(0, SOURCES, BLOCK):
        block = pl.ds(start, BLOCK)
        code = code_ref[block, :]
        spin = code >> 3
        above = (code & 2) != 0
        below = (code & 4) != 0
        odd = (spin & 1) == 1
        high = spin >= 2
        match = (code & 1) == site_parity
        ahead = spread(t_up_ref, block, above, first_row)
        behind = spread(t_down_ref, block, below, first_row)
        plus, minus = both(links_f_ref, back_f_ref, 3, ahead, behind)
        relative = [[base_ref[6 * m + k, block, :] for k in range(6)] for m in range(4)]
        for colour in range(3):
            for part in range(2):
                k = 2 * colour + part
                relative[0][k] += jnp.where(match, 0.0, -hopping * plus[colour][part])
                relative[2][k] += jnp.where(match, 0.0, -hopping * minus[colour][part])
        for k in range(6):
            once = [jnp.where(odd, relative[m ^ 1][k], relative[m][k]) for m in range(4)]
            for b in range(4):
                value = jnp.where(high, once[b ^ 2], once[b])
                rows_ref[pl.ds(start * 24 + b * 6 + k, BLOCK, stride=24), :] = value
                rounded = value.astype(jnp.bfloat16)
                at = pl.ds(b * SOURCES + start, BLOCK)
                fields_ref[at, pl.ds(k * SITES, SITES)] = rounded
                at = pl.ds((4 + b) * SOURCES + start, BLOCK)
                turned = rounded if k % 2 else -rounded
                fields_ref[at, pl.ds((k ^ 1) * SITES, SITES)] = turned
    out_ref[...] = rows_ref[...].astype(jnp.bfloat16)
    product = None
    for k in range(6):
        term = lax.dot_general(
            vectors_ref[k],
            fields_ref[:, pl.ds(k * SITES, SITES)],
            (((1,), (1,)), ((), ())),
            preferred_element_type=jnp.float32,
        )
        product = term if product is None else product + term
    sums_ref[0] = product[:, : 4 * SOURCES]
    sums_ref[1] = product[:, 4 * SOURCES :]


def pick_sources(pick, vectors, code):
    return pl.pallas_call(
        pick_kernel,
        out_shape=(
            jax.ShapeDtypeStruct((6, SOURCES, SITES), jnp.bfloat16),
            jax.ShapeDtypeStruct((4, 3, SOURCES, SITES), jnp.bfloat16),
        ),
        compiler_params=pltpu.CompilerParams(vmem_limit_bytes=8 * 2**20),
        name="pick",
    )(pick, vectors, code)


def space_part(others, pick, center, y_up, y_down, links, back, clover, code):
    f32 = jnp.float32
    return pl.pallas_call(
        space_kernel,
        out_shape=jax.ShapeDtypeStruct((24, SOURCES, SITES), f32),
        scratch_shapes=[
            pltpu.VMEM((72, SITES), f32),
            pltpu.VMEM((72, SITES), f32),
            pltpu.VMEM((144, SITES), f32),
            pltpu.VMEM((12, SOURCES, SITES), f32),
        ],
        compiler_params=pltpu.CompilerParams(vmem_limit_bytes=16 * 2**20),
        cost_estimate=pl.CostEstimate(
            flops=20_000_000, bytes_accessed=1_200_000, transcendentals=0
        ),
        name="space",
    )(others, pick, center, y_up, y_down, links, back, clover, code)


def time_part(vectors, base, t_up, t_down, links, back, code):
    f32 = jnp.float32
    return pl.pallas_call(
        time_kernel,
        out_shape=(
            jax.ShapeDtypeStruct((SOURCES * 24, SITES), jnp.bfloat16),
            jax.ShapeDtypeStruct((2, EIGEN, 4 * SOURCES), f32),
        ),
        scratch_shapes=[
            pltpu.VMEM((SOURCES * 24, SITES), f32),
            pltpu.VMEM((8 * SOURCES, 6 * SITES), jnp.bfloat16),
            pltpu.VMEM((72, SITES), f32),
            pltpu.VMEM((72, SITES), f32),
        ],
        compiler_params=pltpu.CompilerParams(vmem_limit_bytes=16 * 2**20),
        cost_estimate=pl.CostEstimate(
            flops=60_000_000, bytes_accessed=1_200_000, transcendentals=0
        ),
        name="time",
    )(vectors, base, t_up, t_down, links, back, code)


DOMAIN = ("x", "y", "core")


def ring(count, step, closed=True):
    return [(i, (i + step) % count) for i in range(count) if closed or 0 <= i + step < count]


def body(eigenvectors, gauge_links, back_links, clover, source_eigen, source_spin, source_parity):
    time = lax.axis_index("ta")
    offset = (time + lax.axis_index("x")) & 1
    ends = 2 * (time < 3).astype(jnp.int32) + 4 * (time > 0).astype(jnp.int32)
    eigenvectors, offset, ends = lax.optimization_barrier((eigenvectors, offset, ends))
    code = ((source_parity + offset) & 1) + ends + 8 * source_spin
    code = jnp.broadcast_to(code[:, None], (SOURCES, SITES)).astype(jnp.int32)
    row_of = (source_eigen % 32) * 4 + source_eigen // 32
    pick = row_of[:, None] == jnp.arange(EIGEN, dtype=jnp.int32)[None]
    pick = pick.astype(jnp.bfloat16)
    links, back, clover = (
        gauge_links.reshape(72, SITES),
        back_links.reshape(72, SITES),
        clover.reshape(144, SITES),
    )
    cells = eigenvectors.reshape(6, 16, 8, SITES).transpose(1, 0, 2, 3)
    slabs = jnp.stack(
        [
            jnp.concatenate(
                [cells[(4 * h - 1) % 16][None], cells[4 * h : 4 * h + 4], cells[(4 * h + 4) % 16][None]]
            )
            for h in range(4)
        ]
    )
    slabs = lax.all_to_all(slabs, "zh", split_axis=0, concat_axis=0, tiled=True)
    slabs = slabs.transpose(1, 3, 2, 0, 4).reshape(6, 8, 24, SITES)
    pieces = jnp.stack([slabs[1:5], slabs[:4], slabs[2:]], axis=2).reshape(32, 72, SITES)
    pieces = lax.all_to_all(pieces, DOMAIN, split_axis=0, concat_axis=0, tiled=True)
    pieces = pieces.reshape(32, 18, 4, SITES)
    vectors = pieces[:, :6].transpose(1, 0, 2, 3).reshape(6, EIGEN, SITES)
    others = pieces[:, 6:].transpose(1, 0, 2, 3).reshape(12, EIGEN, SITES)
    center, halved = pick_sources(pick, vectors, code)
    y_up = lax.ppermute(center, ("y", "core"), ring(8, -1))
    y_down = lax.ppermute(center, ("y", "core"), ring(8, 1))
    times = lax.all_to_all(halved, "ta", split_axis=0, concat_axis=0, tiled=True)
    t_up = lax.dynamic_index_in_dim(times, jnp.minimum(time + 1, 3), 0, keepdims=False)
    t_down = lax.dynamic_index_in_dim(times, jnp.maximum(time - 1, 0), 0, keepdims=False)
    halos = [y_up, y_down, t_up, t_down]
    base = space_part(others, pick, center, halos[0], halos[1], links, back, clover, code)
    propagated, sums = time_part(vectors, base, halos[2], halos[3], links, back, code)
    sums = sums.reshape(2, 32, 4, 128).transpose(0, 2, 1, 3)
    parts = lax.all_to_all(sums.reshape(32, 8, 128), DOMAIN, split_axis=0, concat_axis=0, tiled=True)
    part = jnp.sum(parts, axis=0)
    parts = lax.all_to_all(
        jnp.broadcast_to(part[None], (4, 8, 128)), "zh", split_axis=0, concat_axis=0, tiled=True
    )
    part = jnp.sum(parts, axis=0) * (1.0 / math.sqrt(3.0 * 64 * 16 * 16))
    whole = lax.all_to_all(
        jnp.broadcast_to(part[None], (32, 8, 128)), DOMAIN, split_axis=0, concat_axis=0, tiled=True
    )
    return (
        propagated.reshape(SOURCES, 4, 3, 2, 1, 1, SITES),
        whole.reshape(2, 1, EIGEN, 4 * SOURCES),
    )


def solution(mesh):
    split = Mesh(mesh.devices.reshape(4, 4, 4, 4, 2), ("ta", "zh", "x", "y", "core"))
    fields = P(None, None, None, None, "ta", ("zh", "x"), ("y", "core"))
    return jax.shard_map(
        body,
        mesh=split,
        in_specs=(P("ta", ("zh", "x", "y", "core")), fields, fields, fields, P(), P(), P()),
        out_specs=(fields, P(None, "ta")),
        check_vma=False,
    )
```

```python
import math

import jax
import jax.numpy as jnp
from jax import lax
from jax.experimental import pallas as pl
from jax.experimental.pallas import tpu as pltpu
from jax.sharding import Mesh, PartitionSpec as P

hopping = 0.125
SOURCES = 32
EIGEN = 128
SITES = 128
BLOCK = 16


def chosen(pick_ref, vectors_ref, k):
    return jnp.dot(pick_ref[...], vectors_ref[k], preferred_element_type=jnp.float32)


def pick_kernel(pick_ref, vectors_ref, code_ref, center_ref, halved_ref):
    lane = lax.broadcasted_iota(jnp.int32, (SOURCES, SITES), 1)
    match = (code_ref[...] & 1) == ((lane + (lane >> 6)) & 1)
    used = []
    for k in range(6):
        value = chosen(pick_ref, vectors_ref, k)
        center_ref[k] = value.astype(jnp.bfloat16)
        used.append(jnp.where(match, value, pltpu.roll(value, 64, 1)))
    for colour in range(3):
        halved_ref[colour] = jnp.where(lane < 64, used[2 * colour], used[2 * colour + 1]).astype(
            jnp.bfloat16
        )


def colour_forward(ref, direction, real, imag):
    out = []
    for row in range(3):
        re = im = None
        for column in range(3):
            index = ((direction * 3 + row) * 3 + column) * 2
            ur, ui = ref[pl.ds(index, 1), :], ref[pl.ds(index + 1, 1), :]
            a = ur * real[column] - ui * imag[column]
            b = ur * imag[column] + ui * real[column]
            re = a if re is None else re + a
            im = b if im is None else im + b
        out.append((re, im))
    return out


def colour_backward(ref, direction, real, imag):
    out = []
    for row in range(3):
        re = im = None
        for column in range(3):
            index = ((direction * 3 + column) * 3 + row) * 2
            ur, ui = ref[pl.ds(index, 1), :], ref[pl.ds(index + 1, 1), :]
            a = ur * real[column] + ui * imag[column]
            b = ur * imag[column] - ui * real[column]
            re = a if re is None else re + a
            im = b if im is None else im + b
        out.append((re, im))
    return out


def both(links_ref, back_ref, direction, ahead, behind):
    fwd = colour_forward(links_ref, direction, ahead[0::2], ahead[1::2])
    bwd = colour_backward(back_ref, direction, behind[0::2], behind[1::2])
    plus = [(f[0] + b[0], f[1] + b[1]) for f, b in zip(fwd, bwd)]
    minus = [(b[0] - f[0], b[1] - f[1]) for f, b in zip(fwd, bwd)]
    return plus, minus


def space_kernel(
    others_ref,
    pick_ref,
    center_ref,
    y_up_ref,
    y_down_ref,
    links_ref,
    back_ref,
    clover_ref,
    code_ref,
    base_ref,
    links_f_ref,
    back_f_ref,
    clover_f_ref,
    beside_ref,
):
    for k in range(12):
        beside_ref[k] = chosen(pick_ref, others_ref, k)
    links_f_ref[...] = links_ref[...].astype(jnp.float32)
    back_f_ref[...] = back_ref[...].astype(jnp.float32)
    clover_f_ref[...] = clover_ref[...].astype(jnp.float32)
    lane = lax.broadcasted_iota(jnp.int32, (BLOCK, SITES), 1)
    cell = lane & 63
    first_row = lane < 64
    last_cell = cell == 63
    first_cell = cell == 0
    site_parity = (lane + (lane >> 6)) & 1

    for start in range(0, SOURCES, BLOCK):
        block = pl.ds(start, BLOCK)
        code = code_ref[block, :]
        spin = code >> 3
        odd = (spin & 1) == 1
        high = spin >= 2
        match = (code & 1) == site_parity
        sign_x = jnp.where(high, 1.0, -1.0)
        sign_y = jnp.where(odd == high, -1.0, 1.0)

        def load(ref, first=0):
            return [ref[first + k, block, :].astype(jnp.float32) for k in range(6)]

        center = load(center_ref)
        ahead = [jnp.where(last_cell, pltpu.roll(v, 63, 1), pltpu.roll(v, 127, 1)) for v in center]
        behind = [jnp.where(first_cell, pltpu.roll(v, 65, 1), pltpu.roll(v, 1, 1)) for v in center]
        total, minus = both(links_f_ref, back_f_ref, 0, ahead, behind)
        cross = [(-sign_x * m[1], sign_x * m[0]) for m in minus]
        ahead = [
            pltpu.roll(jnp.where(first_row, n, v), 64, 1) for n, v in zip(load(y_up_ref), center)
        ]
        behind = [
            pltpu.roll(jnp.where(first_row, v, n), 64, 1) for n, v in zip(load(y_down_ref), center)
        ]
        plus, minus = both(links_f_ref, back_f_ref, 1, ahead, behind)
        total = [(s[0] + p[0], s[1] + p[1]) for s, p in zip(total, plus)]
        cross = [(s[0] + sign_y * m[0], s[1] + sign_y * m[1]) for s, m in zip(cross, minus)]
        plus, minus = both(links_f_ref, back_f_ref, 2, load(beside_ref, 6), load(beside_ref))
        total = [(s[0] + p[0], s[1] + p[1]) for s, p in zip(total, plus)]
        along = [(-sign_y * m[1], sign_y * m[0]) for m in minus]
        def clover(block_index, row, column, part):
            index = ((block_index * 6 + row) * 6 + column) * 2 + part
            return clover_f_ref[pl.ds(index, 1), :]

        def clover_of(same, row, column, part):
            def one(half, low):
                line = 3 * low + row if same else 3 * (1 - low) + row
                return clover(half, line, 3 * low + column, part)

            lower = jnp.where(odd, one(0, 1), one(0, 0))
            upper = jnp.where(odd, one(1, 1), one(1, 0))
            return jnp.where(high, upper, lower)

        relative = [[], [], [], []]
        for colour in range(3):
            for same in (True, False):
                re = im = None
                for column in range(3):
                    cr = clover_of(same, colour, column, 0)
                    ci = clover_of(same, colour, column, 1)
                    vr, vi = center[2 * column], center[2 * column + 1]
                    a = cr * vr - ci * vi
                    b = cr * vi + ci * vr
                    re = a if re is None else re + a
                    im = b if im is None else im + b
                if same:
                    re = jnp.where(match, center[2 * colour] + re, -hopping * total[colour][0])
                    im = jnp.where(match, center[2 * colour + 1] + im, -hopping * total[colour][1])
                    relative[0] += [re, im]
                else:
                    relative[1] += [jnp.where(match, re, 0.0), jnp.where(match, im, 0.0)]
            relative[2] += [jnp.where(match, 0.0, -hopping * v) for v in along[colour]]
            relative[3] += [jnp.where(match, 0.0, -hopping * v) for v in cross[colour]]
        for m in range(4):
            for k in range(6):
                base_ref[6 * m + k, block, :] = relative[m][k]


def spread(ref, block, there, first_row):
    out = []
    for colour in range(3):
        value = jnp.where(there, ref[colour, block, :].astype(jnp.float32), 0.0)
        turned = pltpu.roll(value, 64, 1)
        out += [jnp.where(first_row, value, turned), jnp.where(first_row, turned, value)]
    return out


def time_kernel(
    vectors_ref,
    base_ref,
    t_up_ref,
    t_down_ref,
    links_ref,
    back_ref,
    code_ref,
    out_ref,
    sums_ref,
    rows_ref,
    fields_ref,
    links_f_ref,
    back_f_ref,
):
    links_f_ref[...] = links_ref[...].astype(jnp.float32)
    back_f_ref[...] = back_ref[...].astype(jnp.float32)
    lane = lax.broadcasted_iota(jnp.int32, (BLOCK, SITES), 1)
    first_row = lane < 64
    site_parity = (lane + (lane >> 6)) & 1
    for start in range(0, SOURCES, BLOCK):
        block = pl.ds(start, BLOCK)
        code = code_ref[block, :]
        spin = code >> 3
        above = (code & 2) != 0
        below = (code & 4) != 0
        odd = (spin & 1) == 1
        high = spin >= 2
        match = (code & 1) == site_parity
        ahead = spread(t_up_ref, block, above, first_row)
        behind = spread(t_down_ref, block, below, first_row)
        plus, minus = both(links_f_ref, back_f_ref, 3, ahead, behind)
        relative = [[base_ref[6 * m + k, block, :] for k in range(6)] for m in range(4)]
        for colour in range(3):
            for part in range(2):
                k = 2 * colour + part
                relative[0][k] += jnp.where(match, 0.0, -hopping * plus[colour][part])
                relative[2][k] += jnp.where(match, 0.0, -hopping * minus[colour][part])
        for k in range(6):
            once = [jnp.where(odd, relative[m ^ 1][k], relative[m][k]) for m in range(4)]
            for b in range(4):
                value = jnp.where(high, once[b ^ 2], once[b])
                rows_ref[pl.ds(start * 24 + b * 6 + k, BLOCK, stride=24), :] = value
                rounded = value.astype(jnp.bfloat16)
                at = pl.ds(b * SOURCES + start, BLOCK)
                fields_ref[at, pl.ds(k * SITES, SITES)] = rounded
                at = pl.ds((4 + b) * SOURCES + start, BLOCK)
                turned = rounded if k % 2 else -rounded
                fields_ref[at, pl.ds((k ^ 1) * SITES, SITES)] = turned
    out_ref[...] = rows_ref[...].astype(jnp.bfloat16)
    product = None
    for k in range(6):
        term = lax.dot_general(
            vectors_ref[k],
            fields_ref[:, pl.ds(k * SITES, SITES)],
            (((1,), (1,)), ((), ())),
            preferred_element_type=jnp.float32,
        )
        product = term if product is None else product + term
    sums_ref[0] = product[:, : 4 * SOURCES]
    sums_ref[1] = product[:, 4 * SOURCES :]


def pick_sources(pick, vectors, code):
    return pl.pallas_call(
        pick_kernel,
        out_shape=(
            jax.ShapeDtypeStruct((6, SOURCES, SITES), jnp.bfloat16),
            jax.ShapeDtypeStruct((3, SOURCES, SITES), jnp.bfloat16),
        ),
        compiler_params=pltpu.CompilerParams(vmem_limit_bytes=8 * 2**20),
        name="pick",
    )(pick, vectors, code)


def space_part(others, pick, center, y_up, y_down, links, back, clover, code):
    f32 = jnp.float32
    return pl.pallas_call(
        space_kernel,
        out_shape=jax.ShapeDtypeStruct((24, SOURCES, SITES), f32),
        scratch_shapes=[
            pltpu.VMEM((72, SITES), f32),
            pltpu.VMEM((72, SITES), f32),
            pltpu.VMEM((144, SITES), f32),
            pltpu.VMEM((12, SOURCES, SITES), f32),
        ],
        compiler_params=pltpu.CompilerParams(vmem_limit_bytes=16 * 2**20),
        cost_estimate=pl.CostEstimate(
            flops=20_000_000, bytes_accessed=1_200_000, transcendentals=0
        ),
        name="space",
    )(others, pick, center, y_up, y_down, links, back, clover, code)


def time_part(vectors, base, t_up, t_down, links, back, code):
    f32 = jnp.float32
    return pl.pallas_call(
        time_kernel,
        out_shape=(
            jax.ShapeDtypeStruct((SOURCES * 24, SITES), jnp.bfloat16),
            jax.ShapeDtypeStruct((2, EIGEN, 4 * SOURCES), f32),
        ),
        scratch_shapes=[
            pltpu.VMEM((SOURCES * 24, SITES), f32),
            pltpu.VMEM((8 * SOURCES, 6 * SITES), jnp.bfloat16),
            pltpu.VMEM((72, SITES), f32),
            pltpu.VMEM((72, SITES), f32),
        ],
        compiler_params=pltpu.CompilerParams(vmem_limit_bytes=16 * 2**20),
        cost_estimate=pl.CostEstimate(
            flops=60_000_000, bytes_accessed=1_200_000, transcendentals=0
        ),
        name="time",
    )(vectors, base, t_up, t_down, links, back, code)


DOMAIN = ("x", "y", "core")


def ring(count, step, closed=True):
    return [(i, (i + step) % count) for i in range(count) if closed or 0 <= i + step < count]


def body(eigenvectors, gauge_links, back_links, clover, source_eigen, source_spin, source_parity):
    time = lax.axis_index("ta")
    offset = (time + lax.axis_index("x")) & 1
    ends = 2 * (time < 3).astype(jnp.int32) + 4 * (time > 0).astype(jnp.int32)
    eigenvectors, offset, ends = lax.optimization_barrier((eigenvectors, offset, ends))
    code = ((source_parity + offset) & 1) + ends + 8 * source_spin
    code = jnp.broadcast_to(code[:, None], (SOURCES, SITES)).astype(jnp.int32)
    row_of = (source_eigen % 32) * 4 + source_eigen // 32
    pick = row_of[:, None] == jnp.arange(EIGEN, dtype=jnp.int32)[None]
    pick = pick.astype(jnp.bfloat16)
    links, back, clover = (
        gauge_links.reshape(72, SITES),
        back_links.reshape(72, SITES),
        clover.reshape(144, SITES),
    )
    cells = eigenvectors.reshape(6, 16, 8, SITES).transpose(1, 0, 2, 3)
    slabs = jnp.stack(
        [
            jnp.concatenate(
                [cells[(4 * h - 1) % 16][None], cells[4 * h : 4 * h + 4], cells[(4 * h + 4) % 16][None]]
            )
            for h in range(4)
        ]
    )
    slabs = lax.all_to_all(slabs, "zh", split_axis=0, concat_axis=0, tiled=True)
    slabs = slabs.transpose(1, 3, 2, 0, 4).reshape(6, 8, 24, SITES)
    pieces = jnp.stack([slabs[1:5], slabs[:4], slabs[2:]], axis=2).reshape(32, 72, SITES)
    pieces = lax.all_to_all(pieces, DOMAIN, split_axis=0, concat_axis=0, tiled=True)
    pieces = pieces.reshape(32, 18, 4, SITES)
    vectors = pieces[:, :6].transpose(1, 0, 2, 3).reshape(6, EIGEN, SITES)
    others = pieces[:, 6:].transpose(1, 0, 2, 3).reshape(12, EIGEN, SITES)
    center, halved = pick_sources(pick, vectors, code)
    halos = [
        lax.ppermute(center, ("y", "core"), ring(8, -1)),
        lax.ppermute(center, ("y", "core"), ring(8, 1)),
        lax.ppermute(halved, "ta", ring(4, -1, False)),
        lax.ppermute(halved, "ta", ring(4, 1, False)),
    ]
    base = space_part(others, pick, center, halos[0], halos[1], links, back, clover, code)
    propagated, sums = time_part(vectors, base, halos[2], halos[3], links, back, code)
    sums = sums.reshape(2, 32, 4, 128).transpose(0, 2, 1, 3)
    parts = lax.all_to_all(sums.reshape(32, 8, 128), DOMAIN, split_axis=0, concat_axis=0, tiled=True)
    part = jnp.sum(parts, axis=0)
    parts = lax.all_to_all(
        jnp.broadcast_to(part[None], (4, 8, 128)), "zh", split_axis=0, concat_axis=0, tiled=True
    )
    part = jnp.sum(parts, axis=0) * (1.0 / math.sqrt(3.0 * 64 * 16 * 16))
    whole = lax.all_to_all(
        jnp.broadcast_to(part[None], (32, 8, 128)), DOMAIN, split_axis=0, concat_axis=0, tiled=True
    )
    return (
        propagated.reshape(SOURCES, 4, 3, 2, 1, 1, SITES),
        whole.reshape(2, 1, EIGEN, 4 * SOURCES),
    )


def solution(mesh):
    split = Mesh(mesh.devices.reshape(4, 4, 4, 4, 2), ("ta", "zh", "x", "y", "core"))
    fields = P(None, None, None, None, "ta", ("zh", "x"), ("y", "core"))
    return jax.shard_map(
        body,
        mesh=split,
        in_specs=(P("ta", ("zh", "x", "y", "core")), fields, fields, fields, P(), P(), P()),
        out_specs=(fields, P(None, "ta")),
        check_vma=False,
    )
```
